128 devices in a mesh: ctx: 16 (over z, y), tp: 8 (over x, core).
Axes of the slice: x: 4, y: 4, z: 4, core: 2. Of those that a mesh axis runs over, the one named last changes fastest.
Arguments:
- queries: bfloat16 [16384, 2048], P('ctx', 'tp'), may hold values from -6 to 6
- keys: bfloat16 [16384, 2048], P('ctx', 'tp'), may hold values from -6 to 6
- values: bfloat16 [16384, 4096], P('ctx', 'tp'), may hold values from -6 to 6
- grad_out: bfloat16 [16384, 4096], P('ctx', 'tp'), may hold values from -6 to 6
- input_gate: float32 [8, 16384], P('tp', 'ctx'), may hold values from -6 to 260
- forget_gate: float32 [8, 16384], P('tp', 'ctx'), may hold values from 0 to 12
- query_weight: bfloat16 [4096, 2048], P(None, 'tp'), may hold values from -0.09375 to 0.09375
- key_weight: bfloat16 [4096, 2048], P(None, 'tp'), may hold values from -0.09375 to 0.09375
- value_weight: bfloat16 [4096, 4096], P(None, 'tp'), may hold values from -0.09375 to 0.09375
Outputs:
- token_grad: bfloat16 [16384, 4096], P(('ctx', 'tp'))
- input_gate_grad: float32 [8, 16384], P('tp', 'ctx')
- forget_gate_grad: float32 [8, 16384], P('tp', 'ctx')
The draws below stay inside these ranges and needn't reach their ends.
All inputs are finite; a program needn't handle non-finite values.
Results may differ from the reference program's by a relative error of at most 0.035.
Values may be sent and summed in bfloat16 or wider, within the bound.
A program may use at most 128 MiB of HBM per device.

```python
import math
import jax
import jax.numpy as jnp
from jax import lax

D = 4096
H = 8
DK = 256
DV = 512
TOK_DEV = 1024
TOKENS = 16384


def draw_input_gate(key, part):
    key = jax.random.fold_in(key, 11)
    base_key = jax.random.fold_in(key, 0)
    return jnp.clip(2.0 * jax.random.normal(base_key, (H, TOKENS), jnp.float32), -6.0, 6.0)


def draw_forget_gate(key, part):
    key = jax.random.fold_in(key, 23)
    kind_key, pick_key, rough_key, block_key, spot_key, depth_key = jax.random.split(key, 6)
    slow_share = 0.5
    chosen = jax.random.randint(pick_key, (), 0, H)
    slow = (jax.random.uniform(kind_key, (H, 1), jnp.float32) < slow_share) | (jnp.arange(H)[:, None] == chosen)
    per_step = jnp.where(slow, 0.5 / TOKENS, 1.0 / 40.0)
    rough = jnp.exp(jax.random.uniform(rough_key, (H, TOKENS), jnp.float32, -0.7, 0.7))
    blocks = jnp.exp(jax.random.uniform(block_key, (H, TOKENS // TOK_DEV, 1), jnp.float32, -0.7, 0.7))
    blocks = jnp.broadcast_to(blocks, (H, TOKENS // TOK_DEV, TOK_DEV)).reshape(H, TOKENS)
    rate = jnp.maximum(per_step * rough * blocks, 6.2e-06)
    spots = jax.random.randint(spot_key, (H, 2), 0, TOKENS)
    keep = jax.random.uniform(depth_key, (H, 2), jnp.float32, 0.5, 0.8)
    positions = jnp.arange(TOKENS)[None, :]
    for slot in range(2):
        rate = jnp.where(positions == spots[:, slot:slot + 1], -jnp.log(keep[:, slot:slot + 1]), rate)
    return -jnp.log(jnp.expm1(rate))


def level_of(stream_key, extent, shards, least, largest):
    factor_of = 1.0
    for dim, parts in shards:
        draws = jax.random.uniform(jax.random.fold_in(jax.random.fold_in(stream_key, 6), dim), (parts,), jnp.float32, least / len(shards), largest / len(shards))
        factor_of = factor_of * jnp.repeat(jnp.exp(draws), extent[dim] // parts).reshape((-1,) + (1,) * (len(extent) - 1 - dim))
    return factor_of


def normal_values(key, shape, width, most, cuts=(), held_as=jnp.bfloat16):
    factor_of = level_of(key, shape, cuts, -0.22, 0.18) if cuts else 1.0
    values = jax.random.normal(key, shape, jnp.float32) * width * factor_of
    return jnp.minimum(jnp.maximum(values, -most), most).astype(held_as)


def setup_inputs(seed: int = 0) -> dict:
    arg_keys = jax.random.split(jax.random.key(seed), 10)
    queries = normal_values(arg_keys[0], (TOKENS, H * DK), 1.0, 6.0, ((0, 16), (1, 8)))
    keys = normal_values(arg_keys[1], (TOKENS, H * DK), 1.0, 6.0, ((0, 16), (1, 8)))
    values = normal_values(arg_keys[2], (TOKENS, H * DV), 1.0, 6.0, ((0, 16), (1, 8)))
    grad_out = normal_values(arg_keys[3], (TOKENS, H * DV), 1.0, 6.0, ((0, 16), (1, 8)))
    input_gate = draw_input_gate(jax.random.fold_in(arg_keys[9], 71), 0)
    forget_gate = draw_forget_gate(jax.random.fold_in(arg_keys[9], 71), 0)
    query_weight = normal_values(arg_keys[6], (D, H * DK), D ** -0.5, 0.09375, ((1, 8),))
    key_weight = normal_values(arg_keys[7], (D, H * DK), D ** -0.5, 0.09375, ((1, 8),))
    value_weight = normal_values(arg_keys[8], (D, H * DV), D ** -0.5, 0.09375, ((1, 8),))
    return dict(queries=queries, keys=keys, values=values, grad_out=grad_out, input_gate=input_gate, forget_gate=forget_gate, query_weight=query_weight, key_weight=key_weight, value_weight=value_weight)


HIGH = lax.Precision.HIGHEST
FLOOR = -1e+30

def join_states(earlier, later):
    early_state, early_norm, early_peak, early_total = earlier
    late_state, late_norm, late_peak, late_total = later
    shifted = early_peak + late_total
    peak = jnp.maximum(shifted, late_peak)
    old_scale = jnp.exp(shifted - peak)
    new_scale = jnp.exp(late_peak - peak)
    state = old_scale[..., None, None] * early_state + new_scale[..., None, None] * late_state
    norm_vec = old_scale[..., None] * early_norm + new_scale[..., None] * late_norm
    return (state, norm_vec, peak, early_total + late_total)

def own_summary(keys, values, input_gate, forget_gate):
    log_forget = jax.nn.log_sigmoid(forget_gate)
    cumulative = jnp.cumsum(log_forget)
    block_total = cumulative[-1]
    own_log = block_total - cumulative + input_gate
    own_peak = jnp.max(own_log)
    lifted = jnp.exp(own_log - own_peak)
    key_wide = keys.astype(jnp.float32)
    value_wide = values.astype(jnp.float32)
    local_state = jnp.dot((value_wide * lifted[:, None]).T, key_wide, precision=HIGH)
    local_norm = jnp.dot(lifted, key_wide, precision=HIGH)
    return (local_state, local_norm, own_peak, block_total, cumulative, own_log)

def read_out(queries, keys, values, grad_out, input_gate, cumulative, previous_state, previous_norm, previous_peak):
    length = queries.shape[0]
    shrink = 1.0 / math.sqrt(queries.shape[1])
    positions = jnp.arange(length)
    causal = positions[:, None] >= positions[None, :]
    log_decay = jnp.where(causal, cumulative[:, None] - cumulative[None, :] + input_gate[None, :], FLOOR)
    stabilizer = jnp.maximum(lax.optimization_barrier(jnp.max(log_decay, axis=1)), cumulative + previous_peak)
    damping = jnp.where(causal, jnp.exp(log_decay - stabilizer[:, None]), 0.0)
    scores = jnp.dot(queries, keys.T, preferred_element_type=jnp.float32) * shrink
    weights = damping * scores
    weights_low = weights.astype(jnp.bfloat16)
    carried_scale = jnp.exp(cumulative + previous_peak - stabilizer)
    query_wide = queries.astype(jnp.float32)
    carried = jnp.dot(query_wide, previous_state.T, precision=HIGH) * shrink
    carried_norm = jnp.dot(query_wide, previous_norm, precision=HIGH) * shrink
    numerator = jnp.dot(weights_low, values, preferred_element_type=jnp.float32) + carried_scale[:, None] * carried
    denominator = lax.optimization_barrier(jnp.sum(weights, axis=1)) + carried_scale * carried_norm
    divisor = jnp.sqrt(denominator * denominator + 1.0)
    output = numerator / divisor[:, None]
    upstream = grad_out.astype(jnp.float32)
    grad_numerator = upstream / divisor[:, None]
    grad_denominator = -lax.optimization_barrier(jnp.sum(upstream * output, axis=1)) * denominator / (divisor * divisor)
    exponent = cumulative - stabilizer
    grad_peak = jnp.max(exponent)
    lifted = jnp.exp(exponent - grad_peak)
    grad_state = jnp.dot((grad_numerator * lifted[:, None]).T, query_wide, precision=HIGH) * shrink
    grad_norm = jnp.dot(grad_denominator * lifted, query_wide, precision=HIGH) * shrink
    saved = (damping, weights, weights_low, carried_scale, carried, carried_norm, grad_numerator, grad_denominator)
    return (grad_state, grad_norm, grad_peak, saved)

def pull_back(queries, keys, values, forget_gate, own_log, block_total, own_peak, local_state, local_norm, previous_state, previous_norm, previous_peak, after_state, after_norm, after_peak, saved):
    damping, weights, weights_low, carried_scale, carried, carried_norm, grad_numerator, grad_denominator = saved
    shrink = 1.0 / math.sqrt(queries.shape[1])
    grad_low = grad_numerator.astype(jnp.bfloat16)
    pair_grad = jnp.dot(grad_low, values.T, preferred_element_type=jnp.float32) + grad_denominator[:, None]
    score_grad = damping * pair_grad
    log_grad = weights * pair_grad
    score_low = score_grad.astype(jnp.bfloat16)
    key_wide = keys.astype(jnp.float32)
    value_wide = values.astype(jnp.float32)
    reaching = jnp.exp(own_log + after_peak)
    pulled = jnp.dot(key_wide, after_state.T, precision=HIGH)
    carried_back = jnp.dot(grad_numerator, previous_state, precision=HIGH) + grad_denominator[:, None] * previous_norm[None, :]
    query_grad = (jnp.dot(score_low, keys, preferred_element_type=jnp.float32) + carried_scale[:, None] * carried_back) * shrink
    key_grad = jnp.dot(score_low.T, queries, preferred_element_type=jnp.float32) * shrink
    key_grad = key_grad + reaching[:, None] * (jnp.dot(value_wide, after_state, precision=HIGH) + after_norm[None, :])
    value_grad = jnp.dot(weights_low.T, grad_low, preferred_element_type=jnp.float32) + reaching[:, None] * pulled
    input_grad = lax.optimization_barrier(jnp.sum(log_grad, axis=0)) + reaching * (lax.optimization_barrier(jnp.sum(value_wide * pulled, axis=1)) + jnp.dot(key_wide, after_norm, precision=HIGH))
    row_grad = lax.optimization_barrier(jnp.sum(log_grad, axis=1)) + carried_scale * (lax.optimization_barrier(jnp.sum(grad_numerator * carried, axis=1)) + grad_denominator * carried_norm)
    end_peak = jnp.maximum(previous_peak + block_total, own_peak)
    old_scale = jnp.exp(previous_peak + block_total - end_peak)
    new_scale = jnp.exp(own_peak - end_peak)
    end_state = old_scale * previous_state + new_scale * local_state
    end_norm = old_scale * previous_norm + new_scale * local_norm
    link_grad = jnp.exp(end_peak + after_peak) * (jnp.sum(after_state * end_state) + jnp.sum(after_norm * end_norm))
    balance = row_grad - input_grad
    forget_log_grad = jnp.flip(jnp.cumsum(jnp.flip(balance))) + link_grad
    forget_grad = forget_log_grad * jax.nn.sigmoid(-forget_gate)
    return (query_grad.astype(jnp.bfloat16), key_grad.astype(jnp.bfloat16), value_grad.astype(jnp.bfloat16), input_grad, forget_grad)

def head_pass(items):
    queries, keys, values, grad_out, input_gate, forget_gate = items
    local_state, local_norm, own_peak, block_total, cumulative, own_log = jax.vmap(own_summary)(keys, values, input_gate, forget_gate)
    start = (jnp.zeros((DV, DK), jnp.float32), jnp.zeros((DK,), jnp.float32), jnp.asarray(FLOOR, jnp.float32), jnp.asarray(0.0, jnp.float32))

    def forward_step(carry, item):
        return (join_states(carry, item), carry)
    final, before = lax.scan(forward_step, start, (local_state, local_norm, own_peak, block_total))
    previous_state, previous_norm, previous_peak, spent = before

    def summarize(item):
        grad_state, grad_norm, grad_peak, saved = read_out(*item)
        return (grad_state, grad_norm, grad_peak)
    grad_state, grad_norm, grad_peak = lax.map(summarize, (queries, keys, values, grad_out, input_gate, cumulative, previous_state, previous_norm, previous_peak))

    def reverse_step(carry, item):
        return (join_states(carry, item), carry)
    final_back, after = lax.scan(reverse_step, start, (grad_state, grad_norm, grad_peak, block_total), reverse=True)
    after_state, after_norm, after_peak, spent_back = after

    def finish(item):
        query_b, key_b, value_b, grad_b, input_b, forget_b, cumul_b, own_b, total_b, peak_b, state_b, norm_b, prev_state_b, prev_norm_b, prev_peak_b, after_state_b, after_norm_b, after_peak_b = item
        gs, gn, gp, saved = read_out(query_b, key_b, value_b, grad_b, input_b, cumul_b, prev_state_b, prev_norm_b, prev_peak_b)
        return pull_back(query_b, key_b, value_b, forget_b, own_b, total_b, peak_b, state_b, norm_b, prev_state_b, prev_norm_b, prev_peak_b, after_state_b, after_norm_b, after_peak_b, saved)
    return lax.map(finish, (queries, keys, values, grad_out, input_gate, forget_gate, cumulative, own_log, block_total, own_peak, local_state, local_norm, previous_state, previous_norm, previous_peak, after_state, after_norm, after_peak))

def reference(queries, keys, values, grad_out, input_gate, forget_gate, query_weight, key_weight, value_weight):
    blocks = TOKENS // TOK_DEV

    def split(array, size):
        return array.reshape(blocks, TOK_DEV, H, size).transpose(2, 0, 1, 3)
    items = (split(queries, DK), split(keys, DK), split(values, DV), split(grad_out, DV), input_gate.reshape(H, blocks, TOK_DEV), forget_gate.reshape(H, blocks, TOK_DEV))
    query_low, key_low, value_low, input_grad, forget_grad = lax.map(head_pass, items)
    summed = jnp.zeros((TOKENS, D), jnp.float32)
    for head in range(H):
        term = jnp.dot(query_low[head].reshape(TOKENS, DK), query_weight[:, head * DK:(head + 1) * DK].T, preferred_element_type=jnp.float32)
        term = term + jnp.dot(key_low[head].reshape(TOKENS, DK), key_weight[:, head * DK:(head + 1) * DK].T, preferred_element_type=jnp.float32)
        term = term + jnp.dot(value_low[head].reshape(TOKENS, DV), value_weight[:, head * DV:(head + 1) * DV].T, preferred_element_type=jnp.float32)
        rounded = lax.optimization_barrier(term.astype(jnp.bfloat16))
        summed = summed + rounded.astype(jnp.float32)
    return (summed.astype(jnp.bfloat16), input_grad.reshape(H, TOKENS), forget_grad.reshape(H, TOKENS))
```

```python
import functools

import jax
import jax.numpy as jnp
from jax import lax
from jax.experimental import pallas as pl
from jax.experimental.pallas import tpu as pltpu
from jax.sharding import PartitionSpec as P

MESH = pl.DeviceIdType.MESH
HIGH = lax.Precision.HIGHEST
F32 = jnp.float32
BF16 = jnp.bfloat16
FLOOR = -1e30

TOK, DK, DV, WIDTH = 1024, 256, 512, 4096
BLOCKS = 16
PART = DK // BLOCKS
TILE = 256
TILES = TOK // TILE
COLS = 1024
STEPS = 16
HOPS = 12
OWN = TOK // 8


def nn(a, b):
    return lax.dot_general(a, b, (((1,), (0,)), ((), ())), preferred_element_type=F32)


def nt(a, b):
    return lax.dot_general(a, b, (((1,), (1,)), ((), ())), preferred_element_type=F32)


def row_times(row, matrix):
    high = row.astype(BF16).astype(F32)
    middle = (row - high).astype(BF16).astype(F32)
    low = row - high - middle
    at = lax.broadcasted_iota(jnp.int32, (16, row.shape[1]), 0)
    pieces = jnp.where(at == 0, high, jnp.where(at == 1, middle, jnp.where(at == 2, low, 0.0)))
    return jnp.sum(nn(pieces.astype(BF16), matrix), axis=0, keepdims=True)


def twice(a):
    return jnp.concatenate([a, a], axis=1)


def kernel(
    q_hbm, k_hbm, v_hbm, g_hbm, in_ref, forget_ref, wq_hbm, wk_hbm, wv_hbm,
    token_ref, in_grad_ref, forget_grad_ref,
    q, k, v, g, w_all, q_t, k_t, damp, weigh, pair, score_low, weight_low, act,
    fold, row_a, row_b, wide, stat, stat_back, stat_rx, stat_back_rx,
    fwd_a, fwd_b, fwd_peak, fwd_norm, bwd_a, bwd_b, bwd_peak, bwd_norm,
    local, local_low, grad_low, rx_fwd, tx_fwd, before, rx_bwd, tx_bwd, after,
    product, tx_pair, rx_pair, tx_hop, rx_hop,
    load_sem, stat_send, stat_recv, part_send, part_recv,
    pair_send, pair_recv, hop_send, hop_recv,
):
    ctx, tp = lax.axis_index("ctx"), lax.axis_index("tp")
    chip, core = lax.div(tp, 2), lax.rem(tp, 2)

    def each_peer(do):
        lax.fori_loop(1, BLOCKS, lambda d, _: (do(lax.rem(ctx + d, BLOCKS)), 0)[1], 0)

    def neighbour(side):
        return 2 * lax.rem(chip + 1 + 2 * side, 4) + core

    loads = [
        pltpu.make_async_copy(source, target, load_sem.at[i])
        for i, (source, target) in enumerate(
            (
                (k_hbm, k),
                (v_hbm, v),
                (q_hbm, q),
                (g_hbm, g),
                (wq_hbm, w_all.at[:, pl.ds(0, DK)]),
                (wk_hbm, w_all.at[:, pl.ds(DK, DK)]),
                (wv_hbm, w_all.at[:, pl.ds(2 * DK, DV)]),
            )
        )
    ]
    for load in loads:
        load.start()

    barrier = pltpu.get_barrier_semaphore()
    each_peer(
        lambda p: pl.semaphore_signal(barrier, 1, device_id={"ctx": p}, device_id_type=MESH)
    )
    for partner in (2 * chip + 1 - core, neighbour(0), neighbour(1)):
        pl.semaphore_signal(barrier, 1, device_id={"tp": partner}, device_id_type=MESH)

    def to_fold(row):
        for i in range(8):
            fold[i : i + 1, :] = row[:, 128 * i : 128 * i + 128]
        return fold[...]

    def to_row(folded, row_ref):
        fold[...] = folded
        for i in range(8):
            row_ref[:, 128 * i : 128 * i + 128] = fold[i : i + 1, :]
        return row_ref[...]

    lane = lax.broadcasted_iota(jnp.int32, (8, 128), 1)
    line = lax.broadcasted_iota(jnp.int32, (8, 128), 0)
    down = lax.broadcasted_iota(jnp.int32, (128, 128), 0)
    across = lax.broadcasted_iota(jnp.int32, (128, 128), 1)

    forget = forget_ref[...]
    small = jnp.exp(-jnp.abs(forget))
    series = small * (1.0 - small * (0.5 - small * (1.0 / 3.0 - small * 0.25)))
    log_forget = jnp.minimum(forget, 0.0) - jnp.where(
        small < 0.01, series, jnp.log(1.0 + small)
    )
    log_forget = to_fold(log_forget)
    inside = jnp.dot(
        log_forget, (down <= across).astype(F32), precision=HIGH, preferred_element_type=F32
    )
    lines = jnp.broadcast_to(inside[:, 127:128], (8, 128))
    for d in (1, 2, 4):
        lines = lines + jnp.where(line >= d, pltpu.roll(lines, d, 0), 0.0)
    cumulative = inside + jnp.where(line >= 1, pltpu.roll(lines, 1, 0), 0.0)
    total = lines[7:8, 0:1]
    level = to_fold(in_ref[...]) - cumulative
    top = jnp.max(jnp.max(level, axis=1, keepdims=True), axis=0, keepdims=True)
    first = level[0:1, 0:1]
    lift = jnp.exp(to_row(level, row_a) - top)

    loads[0].wait()
    loads[1].wait()
    k_t[...] = k[...].T
    lifted = k_t[...].astype(F32) * lift
    lifted_high = lifted.astype(BF16)
    lifted_low = (lifted - lifted_high.astype(F32)).astype(BF16)
    local[...] = nn(lifted_high, v[...]) + nn(lifted_low, v[...])
    local_low[...] = local[...].astype(BF16)
    stat[...] = jnp.zeros_like(stat)
    stat[0:1, :] = row_times(lift, k[...])
    stat[1:2, :] = jnp.broadcast_to(total + top, (1, DK))
    stat[2:3, :] = jnp.broadcast_to(total, (1, DK))
    stat[3:4, :] = jnp.broadcast_to(first, (1, DK))

    pl.semaphore_wait(barrier, BLOCKS - 1 + 3)

    def rows_of(ref, p):
        return ref.at[pl.ds(pl.multiple_of(p * PART, PART), PART)]

    def stat_copy(p, way, source, target, slot):
        return pltpu.make_async_remote_copy(
            src_ref=source, dst_ref=target.at[slot], send_sem=stat_send.at[way, p],
            recv_sem=stat_recv.at[way, slot], device_id={"ctx": p}, device_id_type=MESH,
        )

    def part_copy(p, way, source, target, slot):
        return pltpu.make_async_remote_copy(
            src_ref=source, dst_ref=target, send_sem=part_send.at[way, p],
            recv_sem=part_recv.at[way, slot], device_id={"ctx": p}, device_id_type=MESH,
        )

    each_peer(lambda p: stat_copy(p, 0, stat, stat_rx, ctx).start())
    each_peer(lambda p: part_copy(p, 0, rows_of(local_low, p), rx_fwd.at[ctx], ctx).start())
    stat_rx[ctx] = stat[...]
    rx_fwd[ctx] = rows_of(local_low, ctx)[...]

    highest = level
    for d in (1, 2, 4, 8, 16, 32, 64):
        highest = jnp.maximum(
            highest, jnp.where(lane >= d, pltpu.roll(highest, d, 1), FLOOR)
        )
    lines = jnp.broadcast_to(highest[:, 127:128], (8, 128))
    for d in (1, 2, 4):
        lines = jnp.maximum(lines, jnp.where(line >= d, pltpu.roll(lines, d, 0), FLOOR))
    highest = jnp.maximum(highest, jnp.where(line >= 1, pltpu.roll(lines, 1, 0), FLOOR))
    peak_row = to_row(highest, row_b)
    for i in range(8):
        wide[128 * i : 128 * i + 128, :] = jnp.broadcast_to(
            row_a[:, 128 * i : 128 * i + 128], (128, 128)
        ).T
    loads[2].wait()
    loads[3].wait()
    q_t[...] = q[...].T * jnp.asarray(0.0625, BF16)

    def span(i):
        return slice(TILE * i, TILE * (i + 1))

    causal = lax.broadcasted_iota(jnp.int32, (TILE, TILE), 0) <= lax.broadcasted_iota(
        jnp.int32, (TILE, TILE), 1
    )

    def read_tiles(j):
        weight_sum = jnp.zeros((1, TILE), F32)
        pair_sum = jnp.zeros((1, TILE), F32)
        for i in range(j + 1):
            scores = nn(k[span(i), :], q_t[:, span(j)])
            pairs = nt(v[span(i), :], g[span(j), :])
            damping = jnp.exp(twice(wide[span(i), :]) - peak_row[:, span(j)])
            if i == j:
                damping = jnp.where(causal, damping, 0.0)
            weights = damping * scores
            weight_sum = weight_sum + jnp.sum(weights, axis=0, keepdims=True)
            pair_sum = pair_sum + jnp.sum(weights * pairs, axis=0, keepdims=True)
            damp[span(i), span(j)] = damping
            weigh[span(i), span(j)] = weights
            pair[span(i), span(j)] = pairs
        return weight_sum, pair_sum

    sums = [read_tiles(0), read_tiles(1)]

    each_peer(lambda p: stat_copy(p, 0, stat, stat_rx, p).wait_recv())

    def peaks_forward(j, peak):
        fwd_peak[j] = peak
        shifted, own = peak + stat_rx[j, 2:3, :], stat_rx[j, 1:2, :]
        later = jnp.maximum(shifted, own)
        fwd_a[j] = jnp.exp(shifted - later)
        fwd_b[j] = jnp.exp(own - later)
        return later

    lax.fori_loop(0, BLOCKS, peaks_forward, jnp.full((1, DK), FLOOR, F32))

    def peaks_backward(step, peak):
        j = BLOCKS - 1 - step
        bwd_peak[j] = peak
        own = -jnp.maximum(stat_rx[j, 3:4, :], fwd_peak[j])
        shifted = peak + stat_rx[j, 2:3, :]
        later = jnp.maximum(shifted, own)
        bwd_a[j] = jnp.exp(shifted - later)
        bwd_b[j] = jnp.exp(own - later)
        return later

    lax.fori_loop(0, BLOCKS, peaks_backward, jnp.full((1, DK), FLOOR, F32))

    each_peer(lambda p: part_copy(p, 0, rows_of(local_low, p), rx_fwd.at[p], p).wait_recv())

    def join_forward(j, carried):
        state, norm = carried
        tx_fwd[j] = state.astype(BF16)
        fwd_norm[j] = norm
        state = twice(fwd_a[j]) * state + twice(fwd_b[j]) * rx_fwd[j].astype(F32)
        return state, fwd_a[j] * norm + fwd_b[j] * stat_rx[j, 0:1, :]

    nothing = (jnp.zeros((PART, DV), F32), jnp.zeros((1, DK), F32))
    lax.fori_loop(0, BLOCKS, join_forward, nothing)
    each_peer(lambda p: part_copy(p, 1, tx_fwd.at[p], rows_of(before, ctx), ctx).start())
    rows_of(before, ctx)[...] = tx_fwd[ctx]

    sums += [read_tiles(2), read_tiles(3)]
    weight_sum = jnp.concatenate([s[0] for s in sums], axis=1)
    pair_sum = jnp.concatenate([s[1] for s in sums], axis=1)
    before_peak = fwd_peak[ctx][:, 0:1]
    before_norm = fwd_norm[ctx]
    stabilizer = jnp.maximum(peak_row, before_peak)
    shrunk = jnp.exp(peak_row - stabilizer)
    carried_scale = jnp.exp(before_peak - stabilizer)
    carried_norm = row_times(before_norm, q_t[...])
    denominator = weight_sum * shrunk + carried_scale * carried_norm
    square = denominator * denominator + 1.0
    inverse = 1.0 / jnp.sqrt(square)

    each_peer(lambda p: part_copy(p, 1, tx_fwd.at[p], rows_of(before, p), p).wait_recv())

    back = nt(before[...], g[...])
    q_wide = q_t[...].astype(F32)
    carried_pair = jnp.sum(back * q_wide, axis=0, keepdims=True)
    inner = (pair_sum * shrunk + carried_scale * carried_pair) * inverse
    grad_denominator = -inner * denominator / square
    lifted_row = jnp.exp(stabilizer[:, 0:1] - stabilizer)
    grad_low[...] = nn((q_wide * (lifted_row * inverse)).astype(BF16), g[...]).astype(BF16)
    stat_back[...] = jnp.zeros_like(stat_back)
    stat_back[0:1, :] = row_times(lifted_row * grad_denominator * 0.0625, q[...])

    each_peer(lambda p: stat_copy(p, 1, stat_back, stat_back_rx, ctx).start())
    each_peer(lambda p: part_copy(p, 2, rows_of(grad_low, p), rx_bwd.at[ctx], ctx).start())
    stat_back_rx[ctx] = stat_back[...]
    rx_bwd[ctx] = rows_of(grad_low, ctx)[...]

    pair_scale = shrunk * inverse
    pair_shift = shrunk * grad_denominator
    for j in range(TILES):
        for i in range(j + 1):
            at = (span(i), span(j))
            score = damp[at] * (pair[at] * pair_scale[:, span(j)] + pair_shift[:, span(j)])
            score_low[at] = score.astype(BF16)
            weight_low[at] = (weigh[at] * pair_scale[:, span(j)]).astype(BF16)

    each_peer(lambda p: stat_copy(p, 1, stat_back, stat_back_rx, p).wait_recv())
    each_peer(lambda p: part_copy(p, 2, rows_of(grad_low, p), rx_bwd.at[p], p).wait_recv())

    def join_backward(step, carried):
        j = BLOCKS - 1 - step
        state, norm = carried
        tx_bwd[j] = state.astype(BF16)
        bwd_norm[j] = norm
        state = twice(bwd_a[j]) * state + twice(bwd_b[j]) * rx_bwd[j].astype(F32)
        return state, bwd_a[j] * norm + bwd_b[j] * stat_back_rx[j, 0:1, :]

    lax.fori_loop(0, BLOCKS, join_backward, nothing)
    each_peer(lambda p: part_copy(p, 3, tx_bwd.at[p], rows_of(after, ctx), ctx).start())
    rows_of(after, ctx)[...] = tx_bwd[ctx]

    norm_column = jnp.broadcast_to(before_norm, (128, DK)).T
    row_sums = []
    for j in range(TILES):
        near = nn(k_t[:, : TILE * (j + 1)], score_low[: TILE * (j + 1), span(j)])
        outer = twice(norm_column) * grad_denominator[:, span(j)]
        query_grad = near + carried_scale[:, span(j)] * (
            back[:, span(j)] * inverse[:, span(j)] + outer
        )
        row_sums.append(jnp.sum(query_grad * q_wide[:, span(j)], axis=0, keepdims=True))
        act[span(j), 0:DK] = (query_grad * 0.0625).T.astype(BF16)
    row_grad = jnp.concatenate(row_sums, axis=1)
    key_near = [
        nn(score_low[span(i), TILE * i :], q[TILE * i :, :]) * 0.0625 for i in range(TILES)
    ]
    value_near = [nn(weight_low[span(i), TILE * i :], g[TILE * i :, :]) for i in range(TILES)]
    end_a, end_b = fwd_a[ctx][:, 0:1], fwd_b[ctx][:, 0:1]
    end_state = end_a * before[...].astype(F32) + end_b * local[...]
    end_norm = end_a * before_norm + end_b * stat[0:1, :]
    after_peak = bwd_peak[ctx][:, 0:1]
    after_norm = bwd_norm[ctx]
    reaching = jnp.exp(wide[...] + (total + after_peak))

    each_peer(lambda p: part_copy(p, 3, tx_bwd.at[p], rows_of(after, p), p).wait_recv())

    for i in range(TILES):
        reach = twice(reaching[span(i), :])
        key_grad = key_near[i] + reach * (nt(v[span(i), :], after[...]) + after_norm)
        act[span(i), DK : 2 * DK] = key_grad.astype(BF16)
        value_grad = value_near[i] + twice(reach) * nn(k[span(i), :], after[...])
        act[span(i), 2 * DK :] = value_grad.astype(BF16)
        both = key_grad * k[span(i), :].astype(F32)
        wide[span(i), :] = both[:, :128] + both[:, 128:]

    for load in loads[4:]:
        load.wait()

    def pair_copy(s):
        return pltpu.make_async_remote_copy(
            src_ref=tx_pair.at[s], dst_ref=rx_pair.at[s], send_sem=pair_send.at[s],
            recv_sem=pair_recv.at[s], device_id={"tp": 2 * chip + 1 - core}, device_id_type=MESH,
        )

    def hop_copy(s):
        return pltpu.make_async_remote_copy(
            src_ref=tx_hop.at[s], dst_ref=rx_hop.at[s], send_sem=hop_send.at[s],
            recv_sem=hop_recv.at[s], device_id={"tp": neighbour(lax.rem(s, 2))},
            device_id_type=MESH,
        )

    def place(s):
        side, part, phase = lax.rem(s, 2), lax.rem(lax.div(s, 2), 2), lax.div(s, 4)
        middle = jnp.where(phase == 1, 1, 0)
        hop = jnp.where(phase == 0, 2, 1 + 2 * side)
        columns = 2 * (side + middle - 2 * side * middle) + part
        last = s >= HOPS
        return jnp.where(last, 0, hop), jnp.where(last, s - HOPS, columns)

    def multiply(s):
        hop, n = place(s)
        rows = pl.ds(pl.multiple_of(lax.rem(chip + hop, 4) * 2 * OWN, 2 * OWN), 2 * OWN)
        slot = lax.rem(s, 2)
        product[slot] = nt(act[rows, :], w_all[pl.ds(pl.multiple_of(n * COLS, COLS), COLS), :])
        other = pl.ds(pl.multiple_of((1 - core) * OWN, OWN), OWN)
        tx_pair[s] = product[slot, other, :].astype(BF16)
        pair_copy(s).start()

    def own_product(s):
        mine = pl.ds(pl.multiple_of(core * OWN, OWN), OWN)
        pair_copy(s).wait_recv()
        return product[lax.rem(s, 2), mine, :] + rx_pair[s].astype(F32)

    def pass_on(s):
        tx_hop[s] = own_product(s).astype(BF16)
        hop_copy(s).start()

    def join_on(s):
        both = own_product(s)
        hop_copy(s - 8).wait_recv()
        tx_hop[s] = (both + rx_hop[s - 8].astype(F32)).astype(BF16)
        hop_copy(s).start()

    def finish(s):
        n = s - HOPS
        half, part = lax.div(n, 2), lax.rem(n, 2)
        both = own_product(s)
        from_left = 8 - 4 * half + 2 * part
        from_right = 5 + 4 * half + 2 * part
        hop_copy(from_left).wait_recv()
        hop_copy(from_right).wait_recv()
        both = both + rx_hop[from_left].astype(F32) + rx_hop[from_right].astype(F32)
        token_ref[:, pl.ds(pl.multiple_of(n * COLS, COLS), COLS)] = both.astype(BF16)

    def run(first_step, last_step, end):
        def body(s, _):
            multiply(s + 1)
            end(s)
            return 0

        lax.fori_loop(first_step, last_step, body, 0)

    multiply(0)
    run(0, 8, pass_on)
    run(8, 12, join_on)

    for i in range(8):
        in_grad_ref[:, 128 * i : 128 * i + 128] = jnp.sum(
            wide[128 * i : 128 * i + 128, :].T, axis=0, keepdims=True
        )
    linked = jnp.sum(
        jnp.sum(end_state * after[...].astype(F32), axis=1, keepdims=True), axis=0, keepdims=True
    ) + jnp.sum(end_norm * after_norm, axis=1, keepdims=True)
    end_peak = jnp.maximum(before_peak + total, total + top)
    link = jnp.exp(end_peak + after_peak) * linked
    balance = to_fold(row_grad - in_grad_ref[...])
    inside = jnp.dot(
        balance, (down >= across).astype(F32), precision=HIGH, preferred_element_type=F32
    )
    lines = jnp.broadcast_to(inside[:, 0:1], (8, 128))
    for d in (1, 2, 4):
        lines = lines + jnp.where(line < 8 - d, pltpu.roll(lines, 8 - d, 0), 0.0)
    later = inside + jnp.where(line < 7, pltpu.roll(lines, 7, 0), 0.0)
    forget_grad_ref[...] = (to_row(later, row_a) + link) / (1.0 + jnp.exp(forget))

    run(12, 15, finish)
    finish(15)

    def sent(p):
        for way, (source, target) in enumerate(((stat, stat_rx), (stat_back, stat_back_rx))):
            stat_copy(p, way, source, target, ctx).wait_send()
        part_copy(p, 0, rows_of(local_low, p), rx_fwd.at[ctx], ctx).wait_send()
        part_copy(p, 1, tx_fwd.at[p], rows_of(before, ctx), ctx).wait_send()
        part_copy(p, 2, rows_of(grad_low, p), rx_bwd.at[ctx], ctx).wait_send()
        part_copy(p, 3, tx_bwd.at[p], rows_of(after, ctx), ctx).wait_send()

    each_peer(sent)
    lax.fori_loop(0, STEPS, lambda s, _: (pair_copy(s).wait_send(), 0)[1], 0)
    lax.fori_loop(0, HOPS, lambda s, _: (hop_copy(s).wait_send(), 0)[1], 0)


def on_device(*arrays):
    vm = pltpu.VMEM
    dma = pltpu.SemaphoreType.DMA
    anywhere = pl.BlockSpec(memory_space=pl.ANY)
    whole = pl.BlockSpec(memory_space=pltpu.VMEM)
    scratch = [
        vm((TOK, DK), BF16), vm((TOK, DK), BF16), vm((TOK, DV), BF16), vm((TOK, DV), BF16),
        vm((WIDTH, 2 * DK + DV), BF16), vm((DK, TOK), BF16), vm((DK, TOK), BF16),
        vm((TOK, TOK), F32), vm((TOK, TOK), F32), vm((TOK, TOK), F32),
        vm((TOK, TOK), BF16), vm((TOK, TOK), BF16), vm((TOK, 2 * DK + DV), BF16),
        vm((8, 128), F32), vm((1, TOK), F32), vm((1, TOK), F32), vm((TOK, 128), F32),
        vm((8, DK), F32), vm((8, DK), F32), vm((BLOCKS, 8, DK), F32), vm((BLOCKS, 8, DK), F32),
        *[vm((BLOCKS, 1, DK), F32) for _ in range(8)],
        vm((DK, DV), F32), vm((DK, DV), BF16), vm((DK, DV), BF16),
        vm((BLOCKS, PART, DV), BF16), vm((BLOCKS, PART, DV), BF16), vm((DK, DV), BF16),
        vm((BLOCKS, PART, DV), BF16), vm((BLOCKS, PART, DV), BF16), vm((DK, DV), BF16),
        vm((2, 2 * OWN, COLS), F32),
        vm((STEPS, OWN, COLS), BF16), vm((STEPS, OWN, COLS), BF16),
        vm((HOPS, OWN, COLS), BF16), vm((HOPS, OWN, COLS), BF16),
        dma((7,)), dma((2, BLOCKS)), dma((2, BLOCKS)), dma((4, BLOCKS)), dma((4, BLOCKS)),
        dma((STEPS,)), dma((STEPS,)), dma((HOPS,)), dma((HOPS,)),
    ]
    return pl.pallas_call(
        kernel,
        out_shape=(
            jax.ShapeDtypeStruct((OWN, WIDTH), BF16),
            jax.ShapeDtypeStruct((1, TOK), F32),
            jax.ShapeDtypeStruct((1, TOK), F32),
        ),
        in_specs=[anywhere] * 4 + [whole] * 2 + [anywhere] * 3,
        out_specs=(whole, whole, whole),
        scratch_shapes=scratch,
        compiler_params=pltpu.CompilerParams(
            collective_id=0, has_side_effects=True, vmem_limit_bytes=60 * 1024 * 1024
        ),
        cost_estimate=pl.CostEstimate(
            flops=16_000_000_000, bytes_accessed=13_000_000, transcendentals=1_000_000
        ),
    )(*arrays)


def solution(mesh):
    block = P("ctx", "tp")
    gate = P("tp", "ctx")
    weight = P(None, "tp")
    return jax.shard_map(
        on_device,
        mesh=mesh,
        in_specs=(block, block, block, block, gate, gate, weight, weight, weight),
        out_specs=(P(("ctx", "tp"), None), gate, gate),
        check_vma=False,
    )
```

```python
import functools

import jax
import jax.numpy as jnp
from jax import lax
from jax.experimental import pallas as pl
from jax.experimental.pallas import tpu as pltpu
from jax.sharding import PartitionSpec as P

MESH = pl.DeviceIdType.MESH
HIGH = lax.Precision.HIGHEST
F32 = jnp.float32
BF16 = jnp.bfloat16
FLOOR = -1e30

TOK, DK, DV, WIDTH = 1024, 256, 512, 4096
BLOCKS = 16
PART = DK // BLOCKS
TILE = 256
TILES = TOK // TILE
COLS = 1024
HOPS = 12
SOON = DK + DV
FAR_FIRST = (10, 6, 14, 9, 11, 2, 8, 5, 7, 13, 15, 1, 3, 4, 12)
OWN = TOK // 8


def nn(a, b):
    return lax.dot_general(a, b, (((1,), (0,)), ((), ())), preferred_element_type=F32)


def nt(a, b):
    return lax.dot_general(a, b, (((1,), (1,)), ((), ())), preferred_element_type=F32)


def row_times(row, matrix):
    high = row.astype(BF16).astype(F32)
    middle = (row - high).astype(BF16).astype(F32)
    low = row - high - middle
    at = lax.broadcasted_iota(jnp.int32, (16, row.shape[1]), 0)
    pieces = jnp.where(at == 0, high, jnp.where(at == 1, middle, jnp.where(at == 2, low, 0.0)))
    return jnp.sum(nn(pieces.astype(BF16), matrix), axis=0, keepdims=True)


def halves(a):
    high = a.astype(BF16)
    return high, (a - high.astype(F32)).astype(BF16)


def twice(a):
    return jnp.concatenate([a, a], axis=1)


def kernel(
    q_hbm, k_hbm, v_hbm, g_hbm, in_hbm, forget_hbm, wq_hbm, wk_hbm, wv_hbm,
    token_ref, gate_grad_ref,
    q, k, v, g, in_ref, forget_ref, w_own, w_pair, q_t, k_t, weigh, pair, score_low, weight_low,
    near_query, near_key, near_value, stage, act_own, act_out, act_pair,
    fold, row_a, row_b, wide, reaching, wide_grad, stat, stat_back, stat_rx, stat_back_rx,
    fwd_a, fwd_b, fwd_peak, fwd_norm, bwd_a, bwd_b, bwd_peak, bwd_share,
    local, grad_state, rx_fwd, tx_fwd, before, rx_bwd, tx_bwd, after, after_high, after_low,
    product, own, tx_hop, rx_hop,
    load_sem, stat_send, stat_recv, part_send, part_recv, weight_send, weight_recv,
    act_send, act_recv, hop_send, hop_recv,
):
    ctx, tp = lax.axis_index("ctx"), lax.axis_index("tp")
    chip, core = lax.div(tp, 2), lax.rem(tp, 2)
    partner = 2 * chip + 1 - core

    def each_peer(do):
        for d in FAR_FIRST:
            do(lax.rem(ctx + d, BLOCKS))

    def neighbour(side):
        return 2 * lax.rem(chip + 1 + 2 * side, 4) + core

    loads = [
        pltpu.make_async_copy(source, target, load_sem.at[i])
        for i, (source, target) in enumerate(
            (
                (k_hbm, k),
                (v_hbm, v),
                (q_hbm, q),
                (g_hbm, g),
                (wq_hbm, w_own.at[:, pl.ds(0, DK)]),
                (wk_hbm, w_own.at[:, pl.ds(SOON, DK)]),
                (wv_hbm, w_own.at[:, pl.ds(DK, DV)]),
                (in_hbm, in_ref),
                (forget_hbm, forget_ref),
            )
        )
    ]
    for i in (8, 7, 0, 1, 2, 3):
        loads[i].start()

    barrier = pltpu.get_barrier_semaphore()
    each_peer(
        lambda p: pl.semaphore_signal(barrier, 1, device_id={"ctx": p}, device_id_type=MESH)
    )
    for other in (partner, neighbour(0), neighbour(1)):
        pl.semaphore_signal(barrier, 1, device_id={"tp": other}, device_id_type=MESH)

    loads[8].wait()
    loads[7].wait()

    def to_fold(row):
        for i in range(8):
            fold[i : i + 1, :] = row[:, 128 * i : 128 * i + 128]
        return fold[...]

    def to_row(folded, row_ref):
        fold[...] = folded
        for i in range(8):
            row_ref[:, 128 * i : 128 * i + 128] = fold[i : i + 1, :]
        return row_ref[...]

    lane = lax.broadcasted_iota(jnp.int32, (8, 128), 1)
    line = lax.broadcasted_iota(jnp.int32, (8, 128), 0)
    down = lax.broadcasted_iota(jnp.int32, (128, 128), 0)
    across = lax.broadcasted_iota(jnp.int32, (128, 128), 1)

    forget = forget_ref[...]
    small = jnp.exp(-jnp.abs(forget))
    series = small * (1.0 - small * (0.5 - small * (1.0 / 3.0 - small * 0.25)))
    log_forget = jnp.minimum(forget, 0.0) - jnp.where(
        small < 0.01, series, jnp.log(1.0 + small)
    )
    log_forget = to_fold(log_forget)
    inside = jnp.dot(
        log_forget, (down <= across).astype(F32), precision=HIGH, preferred_element_type=F32
    )
    lines = jnp.broadcast_to(inside[:, 127:128], (8, 128))
    for d in (1, 2, 4):
        lines = lines + jnp.where(line >= d, pltpu.roll(lines, d, 0), 0.0)
    cumulative = inside + jnp.where(line >= 1, pltpu.roll(lines, 1, 0), 0.0)
    total = lines[7:8, 0:1]
    level = to_fold(in_ref[...]) - cumulative
    top = jnp.max(jnp.max(level, axis=1, keepdims=True), axis=0, keepdims=True)
    first = level[0:1, 0:1]
    lift = jnp.exp(to_row(level, row_a) - top)

    loads[0].wait()
    def put_norm(tile, norm):
        tile[0:1, :] = norm[:, :128]
        tile[1:2, :] = norm[:, 128:]

    def norm_of(tile):
        return jnp.concatenate([tile[0:1, :], tile[1:2, :]], axis=1)

    stat[...] = jnp.zeros_like(stat)
    put_norm(stat, row_times(lift, k[...]))
    stat[2:3, :] = jnp.broadcast_to(total + top, (1, 128))
    stat[3:4, :] = jnp.broadcast_to(total, (1, 128))
    stat[4:5, :] = jnp.broadcast_to(first, (1, 128))

    def rows_of(ref, p):
        return ref.at[pl.ds(pl.multiple_of(p * PART, PART), PART)]

    def stat_copy(p, way, source, target, slot):
        return pltpu.make_async_remote_copy(
            src_ref=source, dst_ref=target.at[slot], send_sem=stat_send.at[way, p],
            recv_sem=stat_recv.at[way, slot], device_id={"ctx": p}, device_id_type=MESH,
        )

    def part_copy(p, way, source, target, slot):
        return pltpu.make_async_remote_copy(
            src_ref=source, dst_ref=target, send_sem=part_send.at[way, p],
            recv_sem=part_recv.at[way, slot], device_id={"ctx": p}, device_id_type=MESH,
        )

    def weight_copy(i):
        rows = pl.ds(pl.multiple_of(i * TOK, TOK), TOK)
        return pltpu.make_async_remote_copy(
            src_ref=w_own.at[rows], dst_ref=w_pair.at[rows], send_sem=weight_send.at[i],
            recv_sem=weight_recv.at[i], device_id={"tp": partner}, device_id_type=MESH,
        )

    pl.semaphore_wait(barrier, BLOCKS - 1 + 3)
    each_peer(lambda p: stat_copy(p, 0, stat, stat_rx, ctx).start())
    stat_rx[ctx] = stat[...]

    k_t[...] = k[...].T
    lifted_high, lifted_low = halves(k_t[...].astype(F32) * lift)
    loads[1].wait()
    local[...] = nn(lifted_high, v[...]) + nn(lifted_low, v[...])
    each_peer(lambda p: part_copy(p, 0, rows_of(local, p), rx_fwd.at[ctx], ctx).start())
    rx_fwd[ctx] = rows_of(local, ctx)[...]

    for load in loads[4:7]:
        load.start()

    highest = level
    for d in (1, 2, 4, 8, 16, 32, 64):
        highest = jnp.maximum(
            highest, jnp.where(lane >= d, pltpu.roll(highest, d, 1), FLOOR)
        )
    lines = jnp.broadcast_to(highest[:, 127:128], (8, 128))
    for d in (1, 2, 4):
        lines = jnp.maximum(lines, jnp.where(line >= d, pltpu.roll(lines, d, 0), FLOOR))
    highest = jnp.maximum(highest, jnp.where(line >= 1, pltpu.roll(lines, 1, 0), FLOOR))
    peak_row = to_row(highest, row_b)
    for i in range(8):
        wide[128 * i : 128 * i + 128, :] = jnp.broadcast_to(
            row_a[:, 128 * i : 128 * i + 128], (128, 128)
        ).T
    loads[2].wait()
    q_t[...] = q[...].T * jnp.asarray(0.0625, BF16)

    def span(i):
        return slice(TILE * i, TILE * (i + 1))

    causal = lax.broadcasted_iota(jnp.int32, (TILE, TILE), 0) <= lax.broadcasted_iota(
        jnp.int32, (TILE, TILE), 1
    )

    def damping_of(i, j):
        damping = jnp.exp(twice(wide[span(i), :]) - peak_row[:, span(j)])
        return jnp.where(causal, damping, 0.0) if i == j else damping

    def weigh_tiles(j):
        total_row = jnp.zeros((1, TILE), F32)
        for i in range(j + 1):
            weights = damping_of(i, j) * nn(k[span(i), :], q_t[:, span(j)])
            total_row = total_row + jnp.sum(weights, axis=0, keepdims=True)
            weigh[span(i), span(j)] = weights
        return total_row

    def pair_tiles(j):
        total_row = jnp.zeros((1, TILE), F32)
        for i in range(j + 1):
            pairs = nt(v[span(i), :], g[span(j), :])
            total_row = total_row + jnp.sum(
                weigh[span(i), span(j)] * pairs, axis=0, keepdims=True
            )
            pair[span(i), span(j)] = pairs
        return total_row

    weight_sum = jnp.concatenate([weigh_tiles(j) for j in range(TILES)], axis=1)
    loads[3].wait()
    pair_sums = [pair_tiles(0), pair_tiles(1)]
    for load in loads[4:7]:
        load.wait()
    lax.fori_loop(0, 4, lambda i, _: (weight_copy(i).start(), 0)[1], 0)

    each_peer(lambda p: stat_copy(p, 0, stat, stat_rx, p).wait_recv())
    peak = jnp.full((1, DK), FLOOR, F32)
    norm = jnp.zeros((1, DK), F32)
    for j in range(BLOCKS):
        fwd_peak[j] = peak
        fwd_norm[j] = norm
        shifted, highest_own = peak + twice(stat_rx[j, 3:4, :]), twice(stat_rx[j, 2:3, :])
        peak = jnp.maximum(shifted, highest_own)
        fwd_a[j] = jnp.exp(shifted - peak)
        fwd_b[j] = jnp.exp(highest_own - peak)
        norm = fwd_a[j] * norm + fwd_b[j] * norm_of(stat_rx[j])
    before_peak = fwd_peak[ctx][:, 0:1]
    before_norm = fwd_norm[ctx]
    stabilizer = jnp.maximum(peak_row, before_peak)
    shrunk = jnp.exp(peak_row - stabilizer)
    carried_scale = jnp.exp(before_peak - stabilizer)
    carried_norm = row_times(before_norm, q_t[...])
    denominator = weight_sum * shrunk + carried_scale * carried_norm
    square = denominator * denominator + 1.0
    inverse = 1.0 / jnp.sqrt(square)
    lifted_row = jnp.exp(stabilizer[:, 0:1] - stabilizer)
    lifted_high, lifted_low = halves(q_t[...].astype(F32) * (lifted_row * inverse))
    grad_state[...] = nn(lifted_high, g[...]) + nn(lifted_low, g[...])
    each_peer(lambda p: part_copy(p, 2, rows_of(grad_state, p), rx_bwd.at[ctx], ctx).start())
    rx_bwd[ctx] = rows_of(grad_state, ctx)[...]

    each_peer(lambda p: part_copy(p, 0, rows_of(local, p), rx_fwd.at[p], p).wait_recv())
    state = jnp.zeros((PART, DV), F32)
    for j in range(BLOCKS):
        tx_fwd[j] = state
        state = twice(fwd_a[j]) * state + twice(fwd_b[j]) * rx_fwd[j]
    each_peer(lambda p: part_copy(p, 1, tx_fwd.at[p], rows_of(before, ctx), ctx).start())
    rows_of(before, ctx)[...] = tx_fwd[ctx]

    peak = jnp.full((1, DK), FLOOR, F32)
    for j in reversed(range(BLOCKS)):
        bwd_peak[j] = peak
        highest_own = -jnp.maximum(twice(stat_rx[j, 4:5, :]), fwd_peak[j])
        shifted = peak + twice(stat_rx[j, 3:4, :])
        peak = jnp.maximum(shifted, highest_own)
        bwd_a[j] = jnp.exp(shifted - peak)
        bwd_b[j] = jnp.exp(highest_own - peak)
    after_peak = bwd_peak[ctx][:, 0:1]
    between = jnp.zeros((1, DK), F32)
    for j in range(BLOCKS):
        later = jnp.where(j > ctx, 1.0, 0.0)
        highest_own = -jnp.maximum(twice(stat_rx[j, 4:5, :]), fwd_peak[j])
        exponent = jnp.where(j > ctx, highest_own + between - after_peak, 0.0)
        bwd_share[j] = later * jnp.exp(exponent)
        between = between + later * twice(stat_rx[j, 3:4, :])
    reaching[...] = jnp.exp(wide[...] + (total + after_peak))

    pair_sums += [pair_tiles(2), pair_tiles(3)]
    pair_sum = jnp.concatenate(pair_sums, axis=1)

    each_peer(lambda p: part_copy(p, 2, rows_of(grad_state, p), rx_bwd.at[p], p).wait_recv())
    state = jnp.zeros((PART, DV), F32)
    for j in reversed(range(BLOCKS)):
        tx_bwd[j] = state
        state = twice(bwd_a[j]) * state + twice(bwd_b[j]) * rx_bwd[j]
    each_peer(lambda p: part_copy(p, 3, tx_bwd.at[p], rows_of(after, ctx), ctx).start())
    rows_of(after, ctx)[...] = tx_bwd[ctx]

    each_peer(lambda p: part_copy(p, 1, tx_fwd.at[p], rows_of(before, p), p).wait_recv())
    before_high, before_low = halves(before[...])
    back = nt(before_high, g[...]) + nt(before_low, g[...])
    q_wide = q_t[...].astype(F32)
    carried_pair = jnp.sum(back * q_wide, axis=0, keepdims=True)
    inner = (pair_sum * shrunk + carried_scale * carried_pair) * inverse
    grad_denominator = -inner * denominator / square
    stat_back[...] = jnp.zeros_like(stat_back)
    put_norm(stat_back, row_times(lifted_row * grad_denominator * 0.0625, q[...]))
    each_peer(lambda p: stat_copy(p, 1, stat_back, stat_back_rx, ctx).start())
    stat_back_rx[ctx] = stat_back[...]

    pair_scale = shrunk * inverse
    pair_shift = shrunk * grad_denominator
    for j in range(TILES):
        for i in range(j + 1):
            at = (span(i), span(j))
            score = damping_of(i, j) * (
                pair[at] * pair_scale[:, span(j)] + pair_shift[:, span(j)]
            )
            score_low[at] = score.astype(BF16)
            weight_low[at] = (weigh[at] * pair_scale[:, span(j)]).astype(BF16)

    norm_column = twice(jnp.broadcast_to(before_norm, (128, DK)).T)
    row_sums = []
    for j in range(TILES):
        near = nn(k_t[:, : TILE * (j + 1)], score_low[: TILE * (j + 1), span(j)])
        query_grad = near + carried_scale[:, span(j)] * (
            back[:, span(j)] * inverse[:, span(j)] + norm_column * grad_denominator[:, span(j)]
        )
        row_sums.append(jnp.sum(query_grad * q_wide[:, span(j)], axis=0, keepdims=True))
        near_query[span(j), :] = (query_grad * 0.0625).T.astype(BF16)
    row_grad = jnp.concatenate(row_sums, axis=1)
    for i in range(TILES):
        near_key[span(i), :] = nn(score_low[span(i), TILE * i :], q[TILE * i :, :]) * 0.0625
        near_value[span(i), :] = nn(weight_low[span(i), TILE * i :], g[TILE * i :, :])

    each_peer(lambda p: part_copy(p, 3, tx_bwd.at[p], rows_of(after, p), p).wait_recv())

    early, late = slice(0, SOON), slice(SOON, SOON + DK)

    def act_copy(slot, part):
        at = (pl.ds(slot * OWN, OWN), pl.ds(part.start, part.stop - part.start))
        sem = slot + 4 * (part.start > 0)
        return pltpu.make_async_remote_copy(
            src_ref=act_out.at[at], dst_ref=act_pair.at[at], send_sem=act_send.at[sem],
            recv_sem=act_recv.at[sem], device_id={"tp": partner}, device_id_type=MESH,
        )

    mine = pl.ds(pl.multiple_of(core * OWN, OWN), OWN)
    others = pl.ds(pl.multiple_of((1 - core) * OWN, OWN), OWN)
    hops = (2, 1, 3, 0)

    def tokens(slot):
        return pl.ds(
            pl.multiple_of(lax.rem(chip + hops[slot], 4) * 2 * OWN, 2 * OWN), 2 * OWN
        )

    def share(slot, part):
        rows = slice(slot * OWN, (slot + 1) * OWN)
        act_out[rows, part] = stage[others, part]
        act_copy(slot, part).start()
        act_own[rows, part] = stage[mine, part]

    def early_gradients(slot):
        rows = tokens(slot)
        reach = twice(twice(reaching[rows, :]))
        value_grad = near_value[rows, :] + reach * (
            nn(k[rows, :], after_high[...]) + nn(k[rows, :], after_low[...])
        )
        stage[:, 0:DK] = near_query[rows, :]
        stage[:, DK:SOON] = value_grad.astype(BF16)
        share(slot, early)
        return nt(v[rows, :], after_high[...]) + nt(v[rows, :], after_low[...])

    def late_gradients(slot, pulled):
        rows = tokens(slot)
        key_grad = near_key[rows, :] + twice(reaching[rows, :]) * (pulled + after_norm)
        stage[:, late] = key_grad.astype(BF16)
        share(slot, late)
        both = key_grad * k[rows, :].astype(F32)
        wide_grad[rows, :] = both[:, :128] + both[:, 128:]

    def hop_copy(s):
        return pltpu.make_async_remote_copy(
            src_ref=tx_hop.at[s], dst_ref=rx_hop.at[s], send_sem=hop_send.at[s],
            recv_sem=hop_recv.at[s], device_id={"tp": neighbour(lax.rem(s, 2))},
            device_id_type=MESH,
        )

    def columns(n):
        return pl.ds(pl.multiple_of(n * COLS, COLS), COLS)

    def multiply(act, weights, slot, n, part):
        rows = pl.ds(pl.multiple_of(slot * OWN, OWN), OWN)
        return nt(act[rows, part], weights[columns(n), part])

    def product_of(slot, n):
        whole = slice(0, SOON + DK)
        first_head = multiply(act_own, w_own, slot, n, whole)
        return first_head + multiply(act_pair, w_pair, slot, n, whole)

    def send(s, value):
        tx_hop[s] = value.astype(BF16)
        hop_copy(s).start()

    def nearest(s, _):
        side = lax.rem(s, 2)
        n = 2 * (1 - side) + lax.div(s - 4, 2)
        send(s, product_of(1 + side, n))
        return 0

    def join(s, _):
        side = lax.rem(s, 2)
        n = 2 * side + lax.div(s - 8, 2)
        product[...] = product_of(1 + side, n)
        hop_copy(s - 8).wait_recv()
        send(s, product[...] + rx_hop[s - 8].astype(F32))
        return 0

    def keep(n, _):
        own[:, columns(n)] = product_of(3, n)
        return 0

    def finish(i, _):
        half, part = lax.rem(i, 2), lax.div(i, 2)
        n = 2 * half + part
        from_left = 8 - 4 * half + 2 * part
        from_right = 5 + 4 * half + 2 * part
        hop_copy(from_left).wait_recv()
        hop_copy(from_right).wait_recv()
        both = rx_hop[from_left].astype(F32) + rx_hop[from_right].astype(F32)
        token_ref[:, columns(n)] = (own[:, columns(n)] + both).astype(BF16)
        return 0

    after_high[...], after_low[...] = halves(after[...])
    pulled = early_gradients(0)
    sums = [multiply(act_own, w_own, 0, n, early) for n in (0, 2)]
    lax.fori_loop(0, 4, lambda i, _: (weight_copy(i).wait_recv(), 0)[1], 0)

    each_peer(lambda p: stat_copy(p, 1, stat_back, stat_back_rx, p).wait_recv())
    after_norm = jnp.zeros((1, DK), F32)
    for j in range(BLOCKS):
        after_norm = after_norm + bwd_share[j] * norm_of(stat_back_rx[j])
    late_gradients(0, pulled)
    sums = [a + multiply(act_own, w_own, 0, n, late) for a, n in zip(sums, (0, 2))]
    act_copy(0, early).wait_recv()
    sums = [a + multiply(act_pair, w_pair, 0, n, early) for a, n in zip(sums, (0, 2))]
    act_copy(0, late).wait_recv()
    for s, n in ((0, 0), (1, 2)):
        send(s, sums[s] + multiply(act_pair, w_pair, 0, n, late))
    for s, n in ((2, 1), (3, 3)):
        send(s, product_of(0, n))
    for slot in (1, 2):
        late_gradients(slot, early_gradients(slot))
    for slot in (1, 2):
        act_copy(slot, early).wait_recv()
        act_copy(slot, late).wait_recv()
    lax.fori_loop(4, 8, nearest, 0)
    late_gradients(3, early_gradients(3))
    lax.fori_loop(8, 12, join, 0)
    act_copy(3, early).wait_recv()
    act_copy(3, late).wait_recv()
    lax.fori_loop(0, 4, keep, 0)

    in_grad_ref, forget_grad_ref = gate_grad_ref.at[0:1], gate_grad_ref.at[1:2]

    for i in range(8):
        in_grad_ref[:, 128 * i : 128 * i + 128] = jnp.sum(
            wide_grad[128 * i : 128 * i + 128, :].T, axis=0, keepdims=True
        )
    end_a, end_b = fwd_a[ctx][:, 0:1], fwd_b[ctx][:, 0:1]
    end_state = end_a * before[...] + end_b * local[...]
    end_norm = end_a * before_norm + end_b * norm_of(stat[...])
    linked = jnp.sum(
        jnp.sum(end_state * after[...], axis=1, keepdims=True), axis=0, keepdims=True
    ) + jnp.sum(end_norm * after_norm, axis=1, keepdims=True)
    end_peak = jnp.maximum(before_peak + total, total + top)
    link = jnp.exp(end_peak + after_peak) * linked
    balance = to_fold(row_grad - in_grad_ref[...])
    inside = jnp.dot(
        balance, (down >= across).astype(F32), precision=HIGH, preferred_element_type=F32
    )
    lines = jnp.broadcast_to(inside[:, 0:1], (8, 128))
    for d in (1, 2, 4):
        lines = lines + jnp.where(line < 8 - d, pltpu.roll(lines, 8 - d, 0), 0.0)
    later_sum = inside + jnp.where(line < 7, pltpu.roll(lines, 7, 0), 0.0)
    forget_grad_ref[...] = (to_row(later_sum, row_a) + link) / (1.0 + jnp.exp(forget))

    lax.fori_loop(0, 4, finish, 0)

    def sent(p):
        for way, (source, target) in enumerate(((stat, stat_rx), (stat_back, stat_back_rx))):
            stat_copy(p, way, source, target, ctx).wait_send()
        part_copy(p, 0, rows_of(local, p), rx_fwd.at[ctx], ctx).wait_send()
        part_copy(p, 1, tx_fwd.at[p], rows_of(before, ctx), ctx).wait_send()
        part_copy(p, 2, rows_of(grad_state, p), rx_bwd.at[ctx], ctx).wait_send()
        part_copy(p, 3, tx_bwd.at[p], rows_of(after, ctx), ctx).wait_send()

    each_peer(sent)
    lax.fori_loop(0, 4, lambda i, _: (weight_copy(i).wait_send(), 0)[1], 0)
    for slot in range(4):
        act_copy(slot, early).wait_send()
        act_copy(slot, late).wait_send()
    lax.fori_loop(0, HOPS, lambda s, _: (hop_copy(s).wait_send(), 0)[1], 0)


def on_device(*arrays):
    vm = pltpu.VMEM
    dma = pltpu.SemaphoreType.DMA
    anywhere = pl.BlockSpec(memory_space=pl.ANY)
    depth = 2 * DK + DV
    scratch = [
        vm((TOK, DK), BF16), vm((TOK, DK), BF16), vm((TOK, DV), BF16), vm((TOK, DV), BF16),
        vm((1, TOK), F32), vm((1, TOK), F32),
        vm((WIDTH, depth), BF16), vm((WIDTH, depth), BF16),
        vm((DK, TOK), BF16), vm((DK, TOK), BF16),
        vm((TOK, TOK), F32), vm((TOK, TOK), F32), vm((TOK, TOK), BF16), vm((TOK, TOK), BF16),
        vm((TOK, DK), BF16), vm((TOK, DK), F32), vm((TOK, DV), F32), vm((2 * OWN, depth), BF16),
        vm((4 * OWN, depth), BF16), vm((4 * OWN, depth), BF16), vm((4 * OWN, depth), BF16),
        vm((8, 128), F32), vm((1, TOK), F32), vm((1, TOK), F32),
        vm((TOK, 128), F32), vm((TOK, 128), F32), vm((TOK, 128), F32),
        vm((8, 128), F32), vm((8, 128), F32), vm((BLOCKS, 8, 128), F32), vm((BLOCKS, 8, 128), F32),
        *[vm((BLOCKS, 1, DK), F32) for _ in range(8)],
        vm((DK, DV), F32), vm((DK, DV), F32),
        vm((BLOCKS, PART, DV), F32), vm((BLOCKS, PART, DV), F32), vm((DK, DV), F32),
        vm((BLOCKS, PART, DV), F32), vm((BLOCKS, PART, DV), F32), vm((DK, DV), F32),
        vm((DK, DV), BF16), vm((DK, DV), BF16),
        vm((OWN, COLS), F32), vm((OWN, WIDTH), F32),
        vm((HOPS, OWN, COLS), BF16), vm((HOPS, OWN, COLS), BF16),
        dma((9,)), dma((2, BLOCKS)), dma((2, BLOCKS)), dma((4, BLOCKS)), dma((4, BLOCKS)),
        dma((4,)), dma((4,)), dma((8,)), dma((8,)), dma((HOPS,)), dma((HOPS,)),
    ]
    shapes = (
        jax.ShapeDtypeStruct((OWN, WIDTH), BF16),
        jax.ShapeDtypeStruct((2, TOK), F32),
    )
    token_grad, gate_grads = pl.pallas_call(
        kernel,
        out_shape=tuple(pltpu.VMEM(a.shape, a.dtype) for a in shapes),
        in_specs=[anywhere] * 9,
        scratch_shapes=scratch,
        compiler_params=pltpu.CompilerParams(
            collective_id=0, has_side_effects=True, vmem_limit_bytes=60 * 1024 * 1024
        ),
        cost_estimate=pl.CostEstimate(
            flops=16_000_000_000, bytes_accessed=13_000_000, transcendentals=1_000_000
        ),
    )(*arrays)
    return token_grad, gate_grads[0:1], gate_grads[1:2]


def solution(mesh):
    block = P("ctx", "tp")
    gate = P("tp", "ctx")
    weight = P(None, "tp")
    return jax.shard_map(
        on_device,
        mesh=mesh,
        in_specs=(block, block, block, block, gate, gate, weight, weight, weight),
        out_specs=(P(("ctx", "tp"), None), gate, gate),
        check_vma=False,
    )
```
